128 devices in a mesh: ctx: 32 (over y, x, core), head: 4 (over z).
Axes of the slice: x: 4, y: 4, z: 4, core: 2. Of those that a mesh axis runs over, the one named last changes fastest.
Arguments:
- queries: bfloat16 [65536, 2048], P(('ctx', 'head')), may hold values from -30 to 30
- keys: bfloat16 [65536, 2048], P(('ctx', 'head')), may hold values from -30 to 30
- values: bfloat16 [65536, 2048], P(('ctx', 'head')), may hold values from -6 to 6
- out_grad: bfloat16 [65536, 2048], P(('ctx', 'head')), may hold values from -6 to 6
- neighbours: int32 [512, 9], replicated, may hold values from 0 to 511, as said below
- counts: int32 [512], replicated, may hold values from 2 to 9
Outputs:
- attn_out: bfloat16 [65536, 2048], P(('ctx', 'head'))
- query_grad: bfloat16 [65536, 2048], P(('ctx', 'head'))
- key_grad: bfloat16 [65536, 2048], P(('ctx', 'head'))
- value_grad: bfloat16 [65536, 2048], P(('ctx', 'head'))
The draws below stay inside these ranges and needn't reach their ends.
Inputs may be any that keep to these rules, and one draw needn't show every extreme that they name: `neighbours`: row b lists, in increasing order, distinct key blocks within 4 blocks of b, b among them, in its first counts[b] slots; the remaining slots hold b.
All inputs are finite; a program needn't handle non-finite values.
Results may differ from the reference program's by a relative error of at most 0.025.
Values may be sent and summed in bfloat16 or wider, within the bound.
No kernel may reach another device: no remote copies, remote signals or barrier semaphores. Data moves between devices by JAX's collectives and lax.ppermute only.
A program may use at most 192 MiB of HBM per device.

```python
import jax
import jax.numpy as jnp
from jax import lax

H = 16
DH = 128
BLK = 128
REACH = 4
MAXNB = 9
TOKENS = 65536


def neighbour_table(source):
    source = jax.random.fold_in(source, 7)
    layer_key, drop_key = jax.random.split(source)
    block_total = TOKENS // BLK
    offsets = jnp.arange(-REACH, REACH + 1, dtype=jnp.int32)
    distance = jnp.abs(offsets)
    basic = (distance == 0) | (distance == 1) | (distance == REACH)
    refined_only = jnp.logical_not(basic)
    layered = jax.random.randint(layer_key, (block_total // 16,), 0, 4) == 0
    layered = layered.at[1].set(True)
    refined = jnp.repeat(layered, 16)
    dropped = (jax.random.randint(drop_key, (block_total, 2 * REACH + 1), 0, 4) == 0) & (distance == REACH)[None, :] & jnp.logical_not(refined)[:, None]
    block_ids = jnp.arange(block_total, dtype=jnp.int32)
    candidate = block_ids[:, None] + offsets[None, :]
    inside = (candidate >= 0) & (candidate < block_total)
    kept = inside & (basic[None, :] & jnp.logical_not(dropped) | refined_only[None, :] & refined[:, None])
    live_count = jnp.sum(kept.astype(jnp.int32), axis=1)
    slot_ids = jnp.arange(2 * REACH + 1, dtype=jnp.int32)[None, :]
    ranking = jnp.where(kept, slot_ids, slot_ids + 2 * REACH + 1)
    order = jnp.argsort(ranking, axis=1, stable=True)
    listed = jnp.take_along_axis(candidate, order, axis=1)
    listed = jnp.where(slot_ids < live_count[:, None], listed, block_ids[:, None])
    return (listed.astype(jnp.int32), live_count.astype(jnp.int32))


def draw_queries(key, part):
    key = jax.random.fold_in(key, 1)
    drawn = jax.random.truncated_normal(key, -6.0, 6.0, (TOKENS, H * DH), jnp.float32)
    return drawn.astype(jnp.bfloat16)


def draw_keys(key, part):
    key = jax.random.fold_in(key, 2)
    drawn = jax.random.truncated_normal(key, -6.0, 6.0, (TOKENS, H * DH), jnp.float32)
    return drawn.astype(jnp.bfloat16)


def draw_neighbours(key, part):
    listed, live_count = neighbour_table(key)
    return listed


def draw_counts(key, part):
    listed, live_count = neighbour_table(key)
    return live_count


def block_levels(stream_key, extent, shards, least, high):
    def one(dim, shards_of):
        draws = jax.random.uniform(jax.random.fold_in(jax.random.fold_in(stream_key, 6), dim), (shards_of,), jnp.float32, least / len(shards), high / len(shards))
        return jnp.repeat(jnp.exp(draws), extent[dim] // shards_of).reshape((-1,) + (1,) * (len(extent) - dim - 1))

    factor_of = one(*shards[0])
    for cut in shards[1:]:
        factor_of = factor_of * one(*cut)
    return factor_of


def centred(key, dims, deviation, limit, cuts=(), kind=jnp.bfloat16):
    array = jax.random.normal(key, dims, jnp.float32) * deviation
    if len(cuts) > 0:
        array = block_levels(key, dims, cuts, -0.22, 0.18) * array
    return jnp.clip(array, min=-limit, max=limit).astype(kind)


def setup_inputs(seed: int = 0) -> dict:
    key_list = jax.random.split(jax.random.key(seed), 7)
    queries = draw_queries(jax.random.fold_in(key_list[6], 71), 0)
    keys = draw_keys(jax.random.fold_in(key_list[6], 71), 0)
    values = centred(key_list[2], (TOKENS, H * DH), 1.0, 6.0, ((0, 128),))
    out_grad = centred(key_list[3], (TOKENS, H * DH), 1.0, 6.0, ((0, 128),))
    neighbours = draw_neighbours(jax.random.fold_in(key_list[6], 71), 0)
    counts = draw_counts(jax.random.fold_in(key_list[6], 71), 0)
    return dict(queries=queries, keys=keys, values=values, out_grad=out_grad, neighbours=neighbours, counts=counts)


masked_score = -1e30


def attend_block(query_rows, key_blocks, value_blocks, grad_rows, live_slots):
    head_count = query_rows.shape[1]
    scale = DH ** -0.5
    scores = jnp.einsum("qhd,mkhd->hqmk", query_rows.astype(jnp.float32), key_blocks.astype(jnp.float32)) * scale
    scores = jnp.where(live_slots[None, None, :, None], scores, masked_score)
    scores = scores.reshape(head_count, query_rows.shape[0], -1)
    highest = jnp.max(scores, axis=-1, keepdims=True)
    log_total = highest + jnp.log(jnp.sum(jnp.exp(scores - highest), axis=-1, keepdims=True))
    weights = jnp.exp(scores - log_total)
    rounded = weights.astype(jnp.bfloat16)
    flat_keys = key_blocks.reshape(-1, head_count, DH)
    flat_values = value_blocks.reshape(-1, head_count, DH)
    output = jnp.einsum("hqj,jhd->qhd", rounded.astype(jnp.float32), flat_values.astype(jnp.float32)).astype(jnp.bfloat16)
    inner_sum = jnp.sum(grad_rows.astype(jnp.float32) * output.astype(jnp.float32), axis=-1).T[:, :, None]
    slope = jnp.einsum("qhd,jhd->hqj", grad_rows.astype(jnp.float32), flat_values.astype(jnp.float32))
    score_grad = (weights * (slope - inner_sum) * scale).astype(jnp.bfloat16)
    query_part = jnp.einsum("hqj,jhd->qhd", score_grad.astype(jnp.float32), flat_keys.astype(jnp.float32)).astype(jnp.bfloat16)
    key_part = jnp.einsum("hqj,qhd->jhd", score_grad.astype(jnp.float32), query_rows.astype(jnp.float32))
    value_part = jnp.einsum("hqj,qhd->jhd", rounded.astype(jnp.float32), grad_rows.astype(jnp.float32))
    return output, query_part, key_part, value_part


def reference(queries, keys, values, out_grad, neighbours, counts):
    block_total = TOKENS // BLK
    columns = H * DH
    query_blocks = queries.reshape(block_total, BLK, H, DH)
    key_blocks = keys.reshape(block_total, BLK, H, DH)
    value_blocks = values.reshape(block_total, BLK, H, DH)
    grad_blocks = out_grad.reshape(block_total, BLK, H, DH)
    slot_ids = jnp.arange(MAXNB, dtype=jnp.int32)

    def one_block(carried, block_id):
        listed = neighbours[block_id]
        live_slots = slot_ids < counts[block_id]
        output, query_part, key_part, value_part = attend_block(query_blocks[block_id], key_blocks[listed], value_blocks[listed], grad_blocks[block_id], live_slots)
        key_sums = carried[0].at[listed].add(key_part.reshape(MAXNB, BLK, columns))
        value_sums = carried[1].at[listed].add(value_part.reshape(MAXNB, BLK, columns))
        return (key_sums, value_sums), (output.reshape(BLK, columns), query_part.reshape(BLK, columns))

    start_sums = (jnp.zeros((block_total, BLK, columns), jnp.float32), jnp.zeros((block_total, BLK, columns), jnp.float32))
    (key_sums, value_sums), (outputs, query_grads) = lax.scan(one_block, start_sums, jnp.arange(block_total, dtype=jnp.int32))
    attn_out = outputs.reshape(TOKENS, columns)
    query_grad = query_grads.reshape(TOKENS, columns)
    key_grad = key_sums.reshape(TOKENS, columns).astype(jnp.bfloat16)
    value_grad = value_sums.reshape(TOKENS, columns).astype(jnp.bfloat16)
    return attn_out, query_grad, key_grad, value_grad
```

```python
import jax
import jax.numpy as jnp
from jax import lax
from jax.experimental import pallas as pl
from jax.experimental.pallas import tpu as pltpu
from jax.sharding import PartitionSpec as P

H = 16
DH = 128
BLK = 128
REACH = 4
ROWS = 512
COLUMNS = H * DH
PAIR = 2 * BLK
PAIRS = ROWS // PAIR
SPAN = 2 * REACH + 2
WINDOW = SPAN * BLK
EXT = ROWS + 2 * REACH * BLK
AXES = ("ctx", "head")
SCALE = DH ** (-0.5)
LOG2_SCALE = SCALE * 1.4426950408889634
masked_score = -1e30

CUTS = ((0, 4), (4, 12))
GROUPS = ((0, 4), (4, 4), (8, 4), (12, 4))

f32 = jnp.float32
bf16 = jnp.bfloat16


def passed_along(value, steps):
    count = lax.axis_size(AXES)
    initial, last = (max(0, -steps), min(count, count - steps))
    return lax.ppermute(value, AXES, [(source, source + steps) for source in range(initial, last)])


def dot(left, right):
    return lax.dot_general(left, right, (((1,), (0,)), ((), ())), preferred_element_type=f32)


def dot_nt(left, right):
    return lax.dot_general(left, right, (((1,), (1,)), ((), ())), preferred_element_type=f32)


def head_kernel(
    bias_ref, q_ref, g_ref, k_ref, v_ref, kl_ref, ku_ref, vl_ref, vu_ref, *rest
):
    out_ref, dq_ref, own_ref, down_ref, up_ref, kx, vx, kt, vt, ex, eb, ds, dk, dv = rest[-14:]
    sources = ((kl_ref, vl_ref), (k_ref, v_ref), (ku_ref, vu_ref))
    for part, (source_k, source_v) in enumerate(sources):
        rows = pl.ds(part * ROWS, ROWS)
        kx[rows, :] = source_k[...]
        vx[rows, :] = source_v[...]
        kt[:, rows] = source_k[...].T
        vt[:, rows] = source_v[...].T
    for pair in range(PAIRS):
        rows = pl.ds(pair * PAIR, PAIR)
        q = q_ref[rows, :]
        qt = q.T
        gt = g_ref[rows, :].T.astype(f32)
        highest = None
        for slot in range(SPAN):
            here = pl.ds(slot * BLK, BLK)
            there = pl.ds(pair * PAIR + slot * BLK, BLK)
            score = dot(kx[there, :], qt) * LOG2_SCALE + bias_ref[pair, pl.ds(slot, 1), :]
            ex[here, :] = score
            top = jnp.max(score.reshape(BLK // 8, 8, PAIR), axis=0)
            highest = top if highest is None else jnp.maximum(highest, top)
        highest = jnp.max(highest, axis=0, keepdims=True)
        total = None
        for slot in range(SPAN):
            here = pl.ds(slot * BLK, BLK)
            weight = jnp.exp2(ex[here, :] - highest)
            ex[here, :] = weight
            eb[here, :] = weight.astype(bf16)
            part = jnp.sum(weight.reshape(BLK // 8, 8, PAIR), axis=0)
            total = part if total is None else total + part
        inverse = 1.0 / jnp.sum(total, axis=0, keepdims=True)
        window = pl.ds(pair * PAIR, WINDOW)
        out_t = dot(vt[:, window], eb[...]) * inverse
        out = out_t.T.astype(bf16)
        out_ref[rows, :] = out
        gt = (gt * inverse).astype(bf16)
        inner = jnp.sum(gt.astype(f32) * out_t.astype(bf16).astype(f32), axis=0, keepdims=True)
        for slot in range(SPAN):
            here = pl.ds(slot * BLK, BLK)
            there = pl.ds(pair * PAIR + slot * BLK, BLK)
            slope = dot(vx[there, :], gt)
            ds[here, :] = (ex[here, :] * (slope - inner)).astype(bf16)
        dq_ref[rows, :] = (dot(kt[:, window], ds[...]) * SCALE).T.astype(bf16)
        for slot in range(SPAN):
            here = pl.ds(slot * BLK, BLK)
            there = pl.ds(pair * PAIR + slot * BLK, BLK)
            key_term = dot(ds[here, :], q) * SCALE
            value_term = dot_nt(eb[here, :], gt)
            if pair > 0 and pair * PAIR + slot * BLK < (pair - 1) * PAIR + WINDOW:
                key_term += dk[there, :]
                value_term += dv[there, :]
            dk[there, :] = key_term
            dv[there, :] = value_term
    for kind, sums in enumerate((dk, dv)):
        down_ref[kind] = sums[pl.ds(0, ROWS), :].astype(bf16)
        own_ref[kind] = sums[pl.ds(ROWS, ROWS), :]
        up_ref[kind] = sums[pl.ds(2 * ROWS, ROWS), :].astype(bf16)


def run_group(first, heads, bias, queries, out_grad, keys, values, halo, done):
    kl, ku, vl, vu, cut_first = halo
    block = (ROWS, DH)
    whole = pl.BlockSpec(block, lambda h: (0, first + h))
    cut = pl.BlockSpec(block, lambda h: (0, first - cut_first + h))
    terms = pl.BlockSpec((2, ROWS, DH), lambda h: (0, 0, h))
    shape = jax.ShapeDtypeStruct((ROWS, COLUMNS), bf16)
    width = heads * DH
    operands = [bias, queries, out_grad, keys, values, kl, ku, vl, vu]
    in_specs = [pl.BlockSpec(bias.shape, lambda h: (0, 0, 0))] + [whole] * 6 + [cut] * 2
    aliases = {}
    if done is not None:
        aliases = {len(operands): 0, len(operands) + 1: 1}
        operands += list(done)
        in_specs += [pl.BlockSpec(memory_space=pl.ANY)] * 2
    return pl.pallas_call(
        head_kernel,
        grid=(heads,),
        in_specs=in_specs,
        out_specs=[whole, whole, terms, terms, terms],
        out_shape=[
            shape,
            shape,
            jax.ShapeDtypeStruct((2, ROWS, width), f32),
            jax.ShapeDtypeStruct((2, ROWS, width), bf16),
            jax.ShapeDtypeStruct((2, ROWS, width), bf16),
        ],
        scratch_shapes=[
            pltpu.VMEM((EXT, DH), bf16),
            pltpu.VMEM((EXT, DH), bf16),
            pltpu.VMEM((DH, EXT), bf16),
            pltpu.VMEM((DH, EXT), bf16),
            pltpu.VMEM((WINDOW, PAIR), f32),
            pltpu.VMEM((WINDOW, PAIR), bf16),
            pltpu.VMEM((WINDOW, PAIR), bf16),
            pltpu.VMEM((EXT, DH), f32),
            pltpu.VMEM((EXT, DH), f32),
        ],
        input_output_aliases=aliases,
        compiler_params=pltpu.CompilerParams(vmem_limit_bytes=56 * 1024 * 1024),
        cost_estimate=pl.CostEstimate(
            flops=heads * 12 * 2 * ROWS * WINDOW * DH * 2,
            bytes_accessed=heads * 20 * ROWS * DH * 2,
            transcendentals=heads * ROWS * WINDOW,
        ),
        name="attend",
    )(*operands)


def sum_kernel(own_ref, low_ref, high_ref, *rest):
    key_ref, value_ref = rest[-2:]
    for kind, ref in enumerate((key_ref, value_ref)):
        total = own_ref[kind] + low_ref[kind].astype(f32) + high_ref[kind].astype(f32)
        ref[...] = total.astype(bf16)


def sum_group(first, heads, own, low, high, done):
    width = heads * DH
    terms = pl.BlockSpec((2, BLK, width), lambda row: (0, row, 0))
    whole = pl.BlockSpec((BLK, width), lambda row: (row, first // heads))
    shape = jax.ShapeDtypeStruct((ROWS, COLUMNS), bf16)
    operands = [own, low, high]
    in_specs = [terms] * 3
    aliases = {}
    if done is not None:
        aliases = {3: 0, 4: 1}
        operands += list(done)
        in_specs += [pl.BlockSpec(memory_space=pl.ANY)] * 2
    return pl.pallas_call(
        sum_kernel,
        grid=(ROWS // BLK,),
        in_specs=in_specs,
        out_specs=[whole, whole],
        out_shape=[shape, shape],
        input_output_aliases=aliases,
        compiler_params=pltpu.CompilerParams(vmem_limit_bytes=16 * 1024 * 1024),
        cost_estimate=pl.CostEstimate(
            flops=heads * ROWS * DH * 4, bytes_accessed=heads * ROWS * DH * 20, transcendentals=0
        ),
        name="total",
    )(*operands)


def live_bias(neighbours, counts, first_block):
    blocks = ROWS // BLK
    listed = lax.dynamic_slice_in_dim(neighbours, first_block, blocks, 0)
    live_count = lax.dynamic_slice_in_dim(counts, first_block, blocks, 0)
    slot_ids = jnp.arange(neighbours.shape[1], dtype=jnp.int32)
    live = slot_ids[None, :] < live_count[:, None]
    window = jnp.arange(SPAN, dtype=jnp.int32)
    base = first_block - REACH + 2 * (jnp.arange(blocks, dtype=jnp.int32) // 2)
    targets = base[:, None] + window[None, :]
    hit = jnp.any((listed[:, None, :] == targets[:, :, None]) & live[:, None, :], axis=-1)
    bias = jnp.where(hit, 0.0, masked_score).astype(f32)
    bias = bias.reshape(PAIRS, 2, SPAN).transpose(0, 2, 1)
    return jnp.broadcast_to(bias[..., None], (PAIRS, SPAN, 2, BLK)).reshape(PAIRS, SPAN, PAIR)


def per_device(queries, keys, values, out_grad, neighbours, counts):
    first_block = (lax.axis_index("ctx") * lax.axis_size("head") + lax.axis_index("head")) * (
        ROWS // BLK
    )
    bias = live_bias(neighbours, counts, first_block)
    kl = passed_along(keys, 1)
    ku = passed_along(keys, -1)
    halos = []
    for first, heads in CUTS:
        part = values[:, first * DH : (first + heads) * DH]
        if first > 0:
            part, kl, ku = lax.optimization_barrier((part, kl, ku))
        halos.append((kl, ku, passed_along(part, 1), passed_along(part, -1), first))
    outs = None
    sums = None
    for first, heads in GROUPS:
        halo = [halo for halo in halos if halo[-1] <= first][-1]
        attn_out, query_grad, own, down, up = run_group(
            first, heads, bias, queries, out_grad, keys, values, halo, outs
        )
        outs = (attn_out, query_grad)
        low = passed_along(up, 1)
        high = passed_along(down, -1)
        sums = sum_group(first, heads, own, low, high, sums)
    return (outs[0], outs[1], sums[0], sums[1])


def solution(mesh):
    rows = P(AXES, None)
    return jax.shard_map(
        per_device,
        mesh=mesh,
        in_specs=(rows, rows, rows, rows, P(), P()),
        out_specs=(rows, rows, rows, rows),
        check_vma=False,
    )
```

```python
import jax
import jax.numpy as jnp
from jax import lax
from jax.experimental import pallas as pl
from jax.experimental.pallas import tpu as pltpu
from jax.sharding import PartitionSpec as P

H = 16
DH = 128
BLK = 128
REACH = 4
ROWS = 512
COLUMNS = H * DH
PAIR = 2 * BLK
PAIRS = ROWS // PAIR
SPAN = 2 * REACH + 2
WINDOW = SPAN * BLK
EXT = ROWS + 2 * REACH * BLK
AXES = ("ctx", "head")
SCALE = DH ** (-0.5)
LOG2_SCALE = SCALE * 1.4426950408889634
masked_score = -1e30

CUTS = ((0, 8), (8, 8))
GROUPS = ((0, 4), (4, 4), (8, 4), (12, 4))

f32 = jnp.float32
bf16 = jnp.bfloat16


def passed_along(value, steps):
    count = lax.axis_size(AXES)
    initial, last = (max(0, -steps), min(count, count - steps))
    return lax.ppermute(value, AXES, [(source, source + steps) for source in range(initial, last)])


def dot(left, right):
    return lax.dot_general(left, right, (((1,), (0,)), ((), ())), preferred_element_type=f32)


def dot_nt(left, right):
    return lax.dot_general(left, right, (((1,), (1,)), ((), ())), preferred_element_type=f32)


def head_kernel(
    bias_ref, q_ref, g_ref, k_ref, v_ref, kl_ref, ku_ref, vl_ref, vu_ref, *rest
):
    out_ref, dq_ref, own_ref, down_ref, up_ref, kx, vx, kt, vt, ex, eb, ds, dk, dv = rest[-14:]
    sources = ((kl_ref, vl_ref), (k_ref, v_ref), (ku_ref, vu_ref))
    for part, (source_k, source_v) in enumerate(sources):
        rows = pl.ds(part * ROWS, ROWS)
        kx[rows, :] = source_k[...]
        vx[rows, :] = source_v[...]
        kt[:, rows] = source_k[...].T
        vt[:, rows] = source_v[...].T
    for pair in range(PAIRS):
        rows = pl.ds(pair * PAIR, PAIR)
        q = q_ref[rows, :]
        qt = q.T
        gt = g_ref[rows, :].T.astype(f32)
        highest = None
        for slot in range(SPAN):
            here = pl.ds(slot * BLK, BLK)
            there = pl.ds(pair * PAIR + slot * BLK, BLK)
            score = dot(kx[there, :], qt) * LOG2_SCALE + bias_ref[pair, pl.ds(slot, 1), :]
            ex[here, :] = score
            top = jnp.max(score.reshape(BLK // 8, 8, PAIR), axis=0)
            highest = top if highest is None else jnp.maximum(highest, top)
        highest = jnp.max(highest, axis=0, keepdims=True)
        total = None
        for slot in range(SPAN):
            here = pl.ds(slot * BLK, BLK)
            weight = jnp.exp2(ex[here, :] - highest)
            ex[here, :] = weight
            eb[here, :] = weight.astype(bf16)
            part = jnp.sum(weight.reshape(BLK // 8, 8, PAIR), axis=0)
            total = part if total is None else total + part
        inverse = 1.0 / jnp.sum(total, axis=0, keepdims=True)
        window = pl.ds(pair * PAIR, WINDOW)
        out_t = dot(vt[:, window], eb[...]) * inverse
        out = out_t.T.astype(bf16)
        out_ref[rows, :] = out
        gt = (gt * inverse).astype(bf16)
        inner = jnp.sum(gt.astype(f32) * out_t.astype(bf16).astype(f32), axis=0, keepdims=True)
        for slot in range(SPAN):
            here = pl.ds(slot * BLK, BLK)
            there = pl.ds(pair * PAIR + slot * BLK, BLK)
            slope = dot(vx[there, :], gt)
            ds[here, :] = (ex[here, :] * (slope - inner)).astype(bf16)
        dq_ref[rows, :] = (dot(kt[:, window], ds[...]) * SCALE).T.astype(bf16)
        for slot in range(SPAN):
            here = pl.ds(slot * BLK, BLK)
            there = pl.ds(pair * PAIR + slot * BLK, BLK)
            key_term = dot(ds[here, :], q) * SCALE
            value_term = dot_nt(eb[here, :], gt)
            if pair > 0 and pair * PAIR + slot * BLK < (pair - 1) * PAIR + WINDOW:
                key_term += dk[there, :]
                value_term += dv[there, :]
            dk[there, :] = key_term
            dv[there, :] = value_term
    for kind, sums in enumerate((dk, dv)):
        down_ref[kind] = sums[pl.ds(0, ROWS), :].astype(bf16)
        own_ref[kind] = sums[pl.ds(ROWS, ROWS), :]
        up_ref[kind] = sums[pl.ds(2 * ROWS, ROWS), :].astype(bf16)


def run_group(first, heads, bias, queries, out_grad, keys, values, halo, done):
    kl, ku, vl, vu, cut_first = halo
    block = (ROWS, DH)
    whole = pl.BlockSpec(block, lambda h: (0, first + h))
    cut = pl.BlockSpec(block, lambda h: (0, first - cut_first + h))
    terms = pl.BlockSpec((2, ROWS, DH), lambda h: (0, 0, h))
    shape = jax.ShapeDtypeStruct((ROWS, COLUMNS), bf16)
    width = heads * DH
    operands = [bias, queries, out_grad, keys, values, kl, ku, vl, vu]
    in_specs = [pl.BlockSpec(bias.shape, lambda h: (0, 0, 0))] + [whole] * 6 + [cut] * 2
    aliases = {}
    if done is not None:
        aliases = {len(operands): 0, len(operands) + 1: 1}
        operands += list(done)
        in_specs += [pl.BlockSpec(memory_space=pl.ANY)] * 2
    return pl.pallas_call(
        head_kernel,
        grid=(heads,),
        in_specs=in_specs,
        out_specs=[whole, whole, terms, terms, terms],
        out_shape=[
            shape,
            shape,
            jax.ShapeDtypeStruct((2, ROWS, width), f32),
            jax.ShapeDtypeStruct((2, ROWS, width), bf16),
            jax.ShapeDtypeStruct((2, ROWS, width), bf16),
        ],
        scratch_shapes=[
            pltpu.VMEM((EXT, DH), bf16),
            pltpu.VMEM((EXT, DH), bf16),
            pltpu.VMEM((DH, EXT), bf16),
            pltpu.VMEM((DH, EXT), bf16),
            pltpu.VMEM((WINDOW, PAIR), f32),
            pltpu.VMEM((WINDOW, PAIR), bf16),
            pltpu.VMEM((WINDOW, PAIR), bf16),
            pltpu.VMEM((EXT, DH), f32),
            pltpu.VMEM((EXT, DH), f32),
        ],
        input_output_aliases=aliases,
        compiler_params=pltpu.CompilerParams(vmem_limit_bytes=56 * 1024 * 1024),
        cost_estimate=pl.CostEstimate(
            flops=heads * 12 * 2 * ROWS * WINDOW * DH * 2,
            bytes_accessed=heads * 20 * ROWS * DH * 2,
            transcendentals=heads * ROWS * WINDOW,
        ),
        name="attend",
    )(*operands)


def sum_kernel(own_ref, low_ref, high_ref, *rest):
    key_ref, value_ref = rest[-2:]
    for kind, ref in enumerate((key_ref, value_ref)):
        total = own_ref[kind] + low_ref[kind].astype(f32) + high_ref[kind].astype(f32)
        ref[...] = total.astype(bf16)


def sum_group(first, heads, own, low, high, done):
    width = heads * DH
    terms = pl.BlockSpec((2, BLK, width), lambda row: (0, row, 0))
    whole = pl.BlockSpec((BLK, width), lambda row: (row, first // heads))
    shape = jax.ShapeDtypeStruct((ROWS, COLUMNS), bf16)
    operands = [own, low, high]
    in_specs = [terms] * 3
    aliases = {}
    if done is not None:
        aliases = {3: 0, 4: 1}
        operands += list(done)
        in_specs += [pl.BlockSpec(memory_space=pl.ANY)] * 2
    return pl.pallas_call(
        sum_kernel,
        grid=(ROWS // BLK,),
        in_specs=in_specs,
        out_specs=[whole, whole],
        out_shape=[shape, shape],
        input_output_aliases=aliases,
        compiler_params=pltpu.CompilerParams(vmem_limit_bytes=16 * 1024 * 1024),
        cost_estimate=pl.CostEstimate(
            flops=heads * ROWS * DH * 4, bytes_accessed=heads * ROWS * DH * 20, transcendentals=0
        ),
        name="total",
    )(*operands)


def live_bias(neighbours, counts, first_block):
    blocks = ROWS // BLK
    listed = lax.dynamic_slice_in_dim(neighbours, first_block, blocks, 0)
    live_count = lax.dynamic_slice_in_dim(counts, first_block, blocks, 0)
    slot_ids = jnp.arange(neighbours.shape[1], dtype=jnp.int32)
    live = slot_ids[None, :] < live_count[:, None]
    window = jnp.arange(SPAN, dtype=jnp.int32)
    base = first_block - REACH + 2 * (jnp.arange(blocks, dtype=jnp.int32) // 2)
    targets = base[:, None] + window[None, :]
    hit = jnp.any((listed[:, None, :] == targets[:, :, None]) & live[:, None, :], axis=-1)
    bias = jnp.where(hit, 0.0, masked_score).astype(f32)
    bias = bias.reshape(PAIRS, 2, SPAN).transpose(0, 2, 1)
    return jnp.broadcast_to(bias[..., None], (PAIRS, SPAN, 2, BLK)).reshape(PAIRS, SPAN, PAIR)


def per_device(queries, keys, values, out_grad, neighbours, counts):
    first_block = (lax.axis_index("ctx") * lax.axis_size("head") + lax.axis_index("head")) * (
        ROWS // BLK
    )
    bias = live_bias(neighbours, counts, first_block)
    kl = passed_along(keys, 1)
    ku = passed_along(keys, -1)
    halos = []
    for first, heads in CUTS:
        part = values[:, first * DH : (first + heads) * DH]
        if first > 0:
            part, kl, ku = lax.optimization_barrier((part, kl, ku))
        halos.append((kl, ku, passed_along(part, 1), passed_along(part, -1), first))
    outs = None
    sums = None
    for first, heads in GROUPS:
        halo = [halo for halo in halos if halo[-1] <= first][-1]
        attn_out, query_grad, own, down, up = run_group(
            first, heads, bias, queries, out_grad, keys, values, halo, outs
        )
        outs = (attn_out, query_grad)
        low = passed_along(up, 1)
        high = passed_along(down, -1)
        sums = sum_group(first, heads, own, low, high, sums)
    return (outs[0], outs[1], sums[0], sums[1])


def solution(mesh):
    rows = P(AXES, None)
    return jax.shard_map(
        per_device,
        mesh=mesh,
        in_specs=(rows, rows, rows, rows, P(), P()),
        out_specs=(rows, rows, rows, rows),
        check_vma=False,
    )
```

```python
import jax
import jax.numpy as jnp
from jax import lax
from jax.experimental import pallas as pl
from jax.experimental.pallas import tpu as pltpu
from jax.sharding import PartitionSpec as P

H = 16
DH = 128
BLK = 128
REACH = 4
ROWS = 512
COLUMNS = H * DH
PAIR = 2 * BLK
PAIRS = ROWS // PAIR
SPAN = 2 * REACH + 2
WINDOW = SPAN * BLK
EXT = ROWS + 2 * REACH * BLK
SLOTS = 2
CHUNK = SLOTS * BLK
LAG = 5
AXES = ("ctx", "head")
SCALE = DH ** (-0.5)
LOG2_SCALE = SCALE * 1.4426950408889634
masked_score = -1e30

CUTS = ((0, 8), (8, 8))
GROUPS = ((0, 4), (4, 4), (8, 4), (12, 4))

f32 = jnp.float32
bf16 = jnp.bfloat16


def passed_along(value, steps):
    count = lax.axis_size(AXES)
    initial, last = (max(0, -steps), min(count, count - steps))
    return lax.ppermute(value, AXES, [(source, source + steps) for source in range(initial, last)])


def dot(left, right):
    return lax.dot_general(left, right, (((1,), (0,)), ((), ())), preferred_element_type=f32)


def head_kernel(
    bias_ref, q_ref, g_ref, k_ref, v_ref, kl_ref, ku_ref, vl_ref, vu_ref, *rest
):
    out_ref, dq_ref, own_ref, down_ref, up_ref, kx, vx, kt, vt, ex, eb, ds, dk, dv = rest[-14:]
    sources = ((kl_ref, vl_ref), (k_ref, v_ref), (ku_ref, vu_ref))
    for part, (source_k, source_v) in enumerate(sources):
        rows = pl.ds(part * ROWS, ROWS)
        kx[rows, :] = source_k[...]
        vx[rows, :] = source_v[...]
        kt[:, rows] = source_k[...].T
        vt[:, rows] = source_v[...].T
    def pair_steps(pair):
        rows = pl.ds(pair * PAIR, PAIR)
        q = q_ref[rows, :]
        qt = q.T
        gt = g_ref[rows, :].T.astype(f32)
        highest = None
        for start in range(0, SPAN, SLOTS):
            here = pl.ds(start * BLK, CHUNK)
            there = pl.ds(pair * PAIR + start * BLK, CHUNK)
            score = dot(kx[there, :], qt) * LOG2_SCALE
            bias = bias_ref[pair, pl.ds(start, SLOTS), :]
            score = score.reshape(SLOTS, BLK, PAIR) + bias[:, None, :]
            score = score.reshape(CHUNK, PAIR)
            ex[pair, here, :] = score
            top = jnp.max(score.reshape(CHUNK // 8, 8, PAIR), axis=0)
            highest = top if highest is None else jnp.maximum(highest, top)
            yield
        highest = jnp.max(highest, axis=0, keepdims=True)
        total = None
        for start in range(0, SPAN, SLOTS):
            here = pl.ds(start * BLK, CHUNK)
            weight = jnp.exp2(ex[pair, here, :] - highest)
            ex[pair, here, :] = weight
            eb[pair, here, :] = weight.astype(bf16)
            part = jnp.sum(weight.reshape(CHUNK // 8, 8, PAIR), axis=0)
            total = part if total is None else total + part
            yield
        inverse = 1.0 / jnp.sum(total, axis=0, keepdims=True)
        window = pl.ds(pair * PAIR, WINDOW)
        out_t = dot(vt[:, window], eb[pair]) * inverse
        out = out_t.T.astype(bf16)
        out_ref[rows, :] = out
        yield
        gt = (gt * inverse).astype(bf16)
        g = gt.T
        inner = jnp.sum(gt.astype(f32) * out_t.astype(bf16).astype(f32), axis=0, keepdims=True)
        for start in range(0, SPAN, SLOTS):
            here = pl.ds(start * BLK, CHUNK)
            there = pl.ds(pair * PAIR + start * BLK, CHUNK)
            slope = dot(vx[there, :], gt)
            ds[pair, here, :] = (ex[pair, here, :] * (slope - inner)).astype(bf16)
            yield
        dq_ref[rows, :] = (dot(kt[:, window], ds[pair]) * SCALE).T.astype(bf16)
        yield
        for start in range(0, SPAN, SLOTS):
            here = pl.ds(start * BLK, CHUNK)
            there = pl.ds(pair * PAIR + start * BLK, CHUNK)
            key_term = dot(ds[pair, here, :], q) * SCALE
            value_term = dot(eb[pair, here, :], g)
            if pair == 0:
                dk[there, :] = key_term
                dv[there, :] = value_term
            else:
                dk[there, :] += key_term
                dv[there, :] += value_term
            yield
        if pair == 0:
            dk[WINDOW:, :] = jnp.zeros((EXT - WINDOW, DH), f32)
            dv[WINDOW:, :] = jnp.zeros((EXT - WINDOW, DH), f32)
    running = [pair_steps(pair) for pair in range(PAIRS)]
    live = running[:1]
    steps = 0
    while live:
        live = [steps_of for steps_of in live if next(steps_of, running) is not running]
        steps += 1
        if steps % LAG == 0 and steps // LAG < PAIRS:
            live.append(running[steps // LAG])

    for kind, sums in enumerate((dk, dv)):
        down_ref[kind] = sums[pl.ds(0, ROWS), :].astype(bf16)
        own_ref[kind] = sums[pl.ds(ROWS, ROWS), :]
        up_ref[kind] = sums[pl.ds(2 * ROWS, ROWS), :].astype(bf16)


def run_group(first, heads, bias, queries, out_grad, keys, values, halo, done):
    kl, ku, vl, vu, cut_first = halo
    block = (ROWS, DH)
    whole = pl.BlockSpec(block, lambda h: (0, first + h))
    cut = pl.BlockSpec(block, lambda h: (0, first - cut_first + h))
    terms = pl.BlockSpec((2, ROWS, DH), lambda h: (0, 0, h))
    shape = jax.ShapeDtypeStruct((ROWS, COLUMNS), bf16)
    width = heads * DH
    operands = [bias, queries, out_grad, keys, values, kl, ku, vl, vu]
    in_specs = [pl.BlockSpec(bias.shape, lambda h: (0, 0, 0))] + [whole] * 6 + [cut] * 2
    aliases = {}
    if done is not None:
        aliases = {len(operands): 0, len(operands) + 1: 1}
        operands += list(done)
        in_specs += [pl.BlockSpec(memory_space=pl.ANY)] * 2
    return pl.pallas_call(
        head_kernel,
        grid=(heads,),
        in_specs=in_specs,
        out_specs=[whole, whole, terms, terms, terms],
        out_shape=[
            shape,
            shape,
            jax.ShapeDtypeStruct((2, ROWS, width), f32),
            jax.ShapeDtypeStruct((2, ROWS, width), bf16),
            jax.ShapeDtypeStruct((2, ROWS, width), bf16),
        ],
        scratch_shapes=[
            pltpu.VMEM((EXT, DH), bf16),
            pltpu.VMEM((EXT, DH), bf16),
            pltpu.VMEM((DH, EXT), bf16),
            pltpu.VMEM((DH, EXT), bf16),
            pltpu.VMEM((PAIRS, WINDOW, PAIR), f32),
            pltpu.VMEM((PAIRS, WINDOW, PAIR), bf16),
            pltpu.VMEM((PAIRS, WINDOW, PAIR), bf16),
            pltpu.VMEM((EXT, DH), f32),
            pltpu.VMEM((EXT, DH), f32),
        ],
        input_output_aliases=aliases,
        compiler_params=pltpu.CompilerParams(vmem_limit_bytes=56 * 1024 * 1024),
        cost_estimate=pl.CostEstimate(
            flops=heads * 12 * 2 * ROWS * WINDOW * DH * 2,
            bytes_accessed=heads * 20 * ROWS * DH * 2,
            transcendentals=heads * ROWS * WINDOW,
        ),
        name="attend",
    )(*operands)


def sum_kernel(own_ref, low_ref, high_ref, *rest):
    key_ref, value_ref = rest[-2:]
    for kind, ref in enumerate((key_ref, value_ref)):
        total = own_ref[kind] + low_ref[kind].astype(f32) + high_ref[kind].astype(f32)
        ref[...] = total.astype(bf16)


def sum_group(first, heads, own, low, high, done):
    width = heads * DH
    terms = pl.BlockSpec((2, BLK, width), lambda row: (0, row, 0))
    whole = pl.BlockSpec((BLK, width), lambda row: (row, first // heads))
    shape = jax.ShapeDtypeStruct((ROWS, COLUMNS), bf16)
    operands = [own, low, high]
    in_specs = [terms] * 3
    aliases = {}
    if done is not None:
        aliases = {3: 0, 4: 1}
        operands += list(done)
        in_specs += [pl.BlockSpec(memory_space=pl.ANY)] * 2
    return pl.pallas_call(
        sum_kernel,
        grid=(ROWS // BLK,),
        in_specs=in_specs,
        out_specs=[whole, whole],
        out_shape=[shape, shape],
        input_output_aliases=aliases,
        compiler_params=pltpu.CompilerParams(vmem_limit_bytes=16 * 1024 * 1024),
        cost_estimate=pl.CostEstimate(
            flops=heads * ROWS * DH * 4, bytes_accessed=heads * ROWS * DH * 20, transcendentals=0
        ),
        name="total",
    )(*operands)


def live_bias(neighbours, counts, first_block):
    blocks = ROWS // BLK
    listed = lax.dynamic_slice_in_dim(neighbours, first_block, blocks, 0)
    live_count = lax.dynamic_slice_in_dim(counts, first_block, blocks, 0)
    slot_ids = jnp.arange(neighbours.shape[1], dtype=jnp.int32)
    live = slot_ids[None, :] < live_count[:, None]
    window = jnp.arange(SPAN, dtype=jnp.int32)
    base = first_block - REACH + 2 * (jnp.arange(blocks, dtype=jnp.int32) // 2)
    targets = base[:, None] + window[None, :]
    hit = jnp.any((listed[:, None, :] == targets[:, :, None]) & live[:, None, :], axis=-1)
    bias = jnp.where(hit, 0.0, masked_score).astype(f32)
    bias = bias.reshape(PAIRS, 2, SPAN).transpose(0, 2, 1)
    return jnp.broadcast_to(bias[..., None], (PAIRS, SPAN, 2, BLK)).reshape(PAIRS, SPAN, PAIR)


def per_device(queries, keys, values, out_grad, neighbours, counts):
    first_block = (lax.axis_index("ctx") * lax.axis_size("head") + lax.axis_index("head")) * (
        ROWS // BLK
    )
    bias = live_bias(neighbours, counts, first_block)
    kl = passed_along(keys, 1)
    ku = passed_along(keys, -1)
    halos = []
    for first, heads in CUTS:
        part = values[:, first * DH : (first + heads) * DH]
        if first > 0:
            part, kl, ku = lax.optimization_barrier((part, kl, ku))
        halos.append((kl, ku, passed_along(part, 1), passed_along(part, -1), first))
    outs = None
    sums = None
    for first, heads in GROUPS:
        halo = [halo for halo in halos if halo[-1] <= first][-1]
        attn_out, query_grad, own, down, up = run_group(
            first, heads, bias, queries, out_grad, keys, values, halo, outs
        )
        outs = (attn_out, query_grad)
        low = passed_along(up, 1)
        high = passed_along(down, -1)
        sums = sum_group(first, heads, own, low, high, sums)
    return (outs[0], outs[1], sums[0], sums[1])


def solution(mesh):
    rows = P(AXES, None)
    return jax.shard_map(
        per_device,
        mesh=mesh,
        in_specs=(rows, rows, rows, rows, P(), P()),
        out_specs=(rows, rows, rows, rows),
        check_vma=False,
    )
```

```python
import jax
import jax.numpy as jnp
from jax import lax
from jax.experimental import pallas as pl
from jax.experimental.pallas import tpu as pltpu
from jax.sharding import PartitionSpec as P

H = 16
DH = 128
BLK = 128
REACH = 4
ROWS = 512
COLUMNS = H * DH
PAIR = 2 * BLK
PAIRS = ROWS // PAIR
SPAN = 2 * REACH + 2
WINDOW = SPAN * BLK
EXT = ROWS + 2 * REACH * BLK
SLOTS = 2
CHUNK = SLOTS * BLK
LAG = 5
AXES = ("ctx", "head")
SCALE = DH ** (-0.5)
LOG2_SCALE = SCALE * 1.4426950408889634
masked_score = -1e30

CUTS = ((0, 8), (8, 8))
GROUPS = ((0, 4), (4, 4), (8, 4), (12, 4))

f32 = jnp.float32
bf16 = jnp.bfloat16


def passed_along(value, steps):
    count = lax.axis_size(AXES)
    initial, last = (max(0, -steps), min(count, count - steps))
    return lax.ppermute(value, AXES, [(source, source + steps) for source in range(initial, last)])


def dot(left, right):
    return lax.dot_general(left, right, (((1,), (0,)), ((), ())), preferred_element_type=f32)


def head_kernel(
    bias_ref, q_ref, g_ref, k_ref, v_ref, kl_ref, ku_ref, vl_ref, vu_ref, *rest
):
    out_ref, dq_ref, own_ref, down_ref, up_ref, kx, vx, kt, vt, ex, eb, ds, dk, dv = rest[-14:]
    sources = ((kl_ref, vl_ref), (k_ref, v_ref), (ku_ref, vu_ref))
    for part, (source_k, source_v) in enumerate(sources):
        rows = pl.ds(part * ROWS, ROWS)
        kx[rows, :] = source_k[...]
        vx[rows, :] = source_v[...]
        kt[:, rows] = source_k[...].T
        vt[:, rows] = source_v[...].T
    def pair_steps(pair):
        rows = pl.ds(pair * PAIR, PAIR)
        q = q_ref[rows, :]
        qt = q.T
        gt = g_ref[rows, :].T.astype(f32)
        highest = None
        for start in range(0, SPAN, SLOTS):
            here = pl.ds(start * BLK, CHUNK)
            there = pl.ds(pair * PAIR + start * BLK, CHUNK)
            score = dot(kx[there, :], qt) * LOG2_SCALE
            bias = bias_ref[pair, pl.ds(start, SLOTS), :]
            score = score.reshape(SLOTS, BLK, PAIR) + bias[:, None, :]
            score = score.reshape(CHUNK, PAIR)
            ex[pair, here, :] = score
            top = jnp.max(score.reshape(CHUNK // 8, 8, PAIR), axis=0)
            highest = top if highest is None else jnp.maximum(highest, top)
            yield
        highest = jnp.max(highest, axis=0, keepdims=True)
        total = None
        for start in range(0, SPAN, SLOTS):
            here = pl.ds(start * BLK, CHUNK)
            weight = jnp.exp2(ex[pair, here, :] - highest)
            ex[pair, here, :] = weight
            eb[pair, here, :] = weight.astype(bf16)
            part = jnp.sum(weight.reshape(CHUNK // 8, 8, PAIR), axis=0)
            total = part if total is None else total + part
            yield
        inverse = 1.0 / jnp.sum(total, axis=0, keepdims=True)
        window = pl.ds(pair * PAIR, WINDOW)
        out_t = dot(vt[:, window], eb[pair]) * inverse
        out = out_t.T.astype(bf16)
        out_ref[rows, :] = out
        yield
        gt = (gt * inverse).astype(bf16)
        g = gt.T
        inner = jnp.sum(gt.astype(f32) * out_t.astype(bf16).astype(f32), axis=0, keepdims=True)
        for start in range(0, SPAN, SLOTS):
            here = pl.ds(start * BLK, CHUNK)
            there = pl.ds(pair * PAIR + start * BLK, CHUNK)
            slope = dot(vx[there, :], gt)
            ds[pair, here, :] = (ex[pair, here, :] * (slope - inner)).astype(bf16)
            yield
        dq_ref[rows, :] = (dot(kt[:, window], ds[pair]) * SCALE).T.astype(bf16)
        yield
        for start in range(0, SPAN, SLOTS):
            here = pl.ds(start * BLK, CHUNK)
            there = pl.ds(pair * PAIR + start * BLK, CHUNK)
            key_term = dot(ds[pair, here, :], q) * SCALE
            value_term = dot(eb[pair, here, :], g)
            if pair == 0:
                dk[there, :] = key_term
                dv[there, :] = value_term
            else:
                dk[there, :] += key_term
                dv[there, :] += value_term
            yield
        if pair == 0:
            dk[WINDOW:, :] = jnp.zeros((EXT - WINDOW, DH), f32)
            dv[WINDOW:, :] = jnp.zeros((EXT - WINDOW, DH), f32)
    running = [pair_steps(pair) for pair in range(PAIRS)]
    live = running[:1]
    steps = 0
    while live:
        live = [steps_of for steps_of in live if next(steps_of, running) is not running]
        steps += 1
        if steps % LAG == 0 and steps // LAG < PAIRS:
            live.append(running[steps // LAG])

    for kind, sums in enumerate((dk, dv)):
        down_ref[kind] = sums[pl.ds(0, ROWS), :].astype(bf16)
        own_ref[kind] = sums[pl.ds(ROWS, ROWS), :]
        up_ref[kind] = sums[pl.ds(2 * ROWS, ROWS), :].astype(bf16)


def run_group(first, heads, bias, queries, out_grad, keys, values, halo, done):
    kl, ku, vl, vu, cut_first = halo
    block = (ROWS, DH)
    whole = pl.BlockSpec(block, lambda h: (0, first + h))
    cut = pl.BlockSpec(block, lambda h: (0, first - cut_first + h))
    terms = pl.BlockSpec((2, ROWS, DH), lambda h: (0, 0, h))
    shape = jax.ShapeDtypeStruct((ROWS, COLUMNS), bf16)
    width = heads * DH
    operands = [bias, queries, out_grad, keys, values, kl, ku, vl, vu]
    in_specs = [pl.BlockSpec(bias.shape, lambda h: (0, 0, 0))] + [whole] * 6 + [cut] * 2
    aliases = {}
    if done is not None:
        aliases = {len(operands): 0, len(operands) + 1: 1}
        operands += list(done)
        in_specs += [pl.BlockSpec(memory_space=pl.ANY)] * 2
    return pl.pallas_call(
        head_kernel,
        grid=(heads,),
        in_specs=in_specs,
        out_specs=[whole, whole, terms, terms, terms],
        out_shape=[
            shape,
            shape,
            jax.ShapeDtypeStruct((2, ROWS, width), f32),
            jax.ShapeDtypeStruct((2, ROWS, width), bf16),
            jax.ShapeDtypeStruct((2, ROWS, width), bf16),
        ],
        scratch_shapes=[
            pltpu.VMEM((EXT, DH), bf16),
            pltpu.VMEM((EXT, DH), bf16),
            pltpu.VMEM((DH, EXT), bf16),
            pltpu.VMEM((DH, EXT), bf16),
            pltpu.VMEM((PAIRS, WINDOW, PAIR), f32),
            pltpu.VMEM((PAIRS, WINDOW, PAIR), bf16),
            pltpu.VMEM((PAIRS, WINDOW, PAIR), bf16),
            pltpu.VMEM((EXT, DH), f32),
            pltpu.VMEM((EXT, DH), f32),
        ],
        input_output_aliases=aliases,
        compiler_params=pltpu.CompilerParams(vmem_limit_bytes=56 * 1024 * 1024),
        cost_estimate=pl.CostEstimate(
            flops=heads * 12 * 2 * ROWS * WINDOW * DH * 2,
            bytes_accessed=heads * 20 * ROWS * DH * 2,
            transcendentals=heads * ROWS * WINDOW,
        ),
        name="attend",
    )(*operands)


def sum_kernel(own_ref, low_ref, high_ref, *rest):
    key_ref, value_ref = rest[-2:]
    for kind, ref in enumerate((key_ref, value_ref)):
        total = own_ref[kind] + low_ref[kind].astype(f32) + high_ref[kind].astype(f32)
        ref[...] = total.astype(bf16)


def sum_group(first, heads, own, low, high, done):
    width = heads * DH
    terms = pl.BlockSpec((2, PAIR, width), lambda row: (0, row, 0))
    whole = pl.BlockSpec((PAIR, width), lambda row: (row, first // heads))
    shape = jax.ShapeDtypeStruct((ROWS, COLUMNS), bf16)
    operands = [own, low, high]
    in_specs = [terms] * 3
    aliases = {}
    if done is not None:
        aliases = {3: 0, 4: 1}
        operands += list(done)
        in_specs += [pl.BlockSpec(memory_space=pl.ANY)] * 2
    return pl.pallas_call(
        sum_kernel,
        grid=(PAIRS,),
        in_specs=in_specs,
        out_specs=[whole, whole],
        out_shape=[shape, shape],
        input_output_aliases=aliases,
        compiler_params=pltpu.CompilerParams(vmem_limit_bytes=16 * 1024 * 1024),
        cost_estimate=pl.CostEstimate(
            flops=heads * ROWS * DH * 4, bytes_accessed=heads * ROWS * DH * 20, transcendentals=0
        ),
        name="total",
    )(*operands)


def live_bias(neighbours, counts, first_block):
    blocks = ROWS // BLK
    listed = lax.dynamic_slice_in_dim(neighbours, first_block, blocks, 0)
    live_count = lax.dynamic_slice_in_dim(counts, first_block, blocks, 0)
    slot_ids = jnp.arange(neighbours.shape[1], dtype=jnp.int32)
    live = slot_ids[None, :] < live_count[:, None]
    window = jnp.arange(SPAN, dtype=jnp.int32)
    base = first_block - REACH + 2 * (jnp.arange(blocks, dtype=jnp.int32) // 2)
    targets = base[:, None] + window[None, :]
    hit = jnp.any((listed[:, None, :] == targets[:, :, None]) & live[:, None, :], axis=-1)
    bias = jnp.where(hit, 0.0, masked_score).astype(f32)
    bias = bias.reshape(PAIRS, 2, SPAN).transpose(0, 2, 1)
    return jnp.broadcast_to(bias[..., None], (PAIRS, SPAN, 2, BLK)).reshape(PAIRS, SPAN, PAIR)


def per_device(queries, keys, values, out_grad, neighbours, counts):
    first_block = (lax.axis_index("ctx") * lax.axis_size("head") + lax.axis_index("head")) * (
        ROWS // BLK
    )
    bias = live_bias(neighbours, counts, first_block)
    kl = passed_along(keys, 1)
    ku = passed_along(keys, -1)
    halos = []
    for first, heads in CUTS:
        part = values[:, first * DH : (first + heads) * DH]
        if first > 0:
            part, kl, ku = lax.optimization_barrier((part, kl, ku))
        halos.append((kl, ku, passed_along(part, 1), passed_along(part, -1), first))
    outs = None
    sums = None
    for first, heads in GROUPS:
        halo = [halo for halo in halos if halo[-1] <= first][-1]
        attn_out, query_grad, own, down, up = run_group(
            first, heads, bias, queries, out_grad, keys, values, halo, outs
        )
        outs = (attn_out, query_grad)
        low = passed_along(up, 1)
        high = passed_along(down, -1)
        sums = sum_group(first, heads, own, low, high, sums)
    return (outs[0], outs[1], sums[0], sums[1])


def solution(mesh):
    rows = P(AXES, None)
    return jax.shard_map(
        per_device,
        mesh=mesh,
        in_specs=(rows, rows, rows, rows, P(), P()),
        out_specs=(rows, rows, rows, rows),
        check_vma=False,
    )
```
